256 devices in a mesh: samp: 64 (over z, y_lo, x), chan: 4 (over y_hi, core).
Axes of the slice: x: 4, y: 4 (y_hi: 2, y_lo: 2; y = y_hi * 2 + y_lo), z: 8, core: 2. Of those that a mesh axis runs over, the one named last changes fastest.
Arguments:
- activations: bfloat16 [50176, 768], P('samp', 'chan'), may hold values from -16 to 16
- gradients: bfloat16 [50176, 3072], P('samp', 'chan'), may hold values from -16 to 16
- basis_act: bfloat16 [768, 768], P(None, 'chan'), may hold values from -0.21875 to 0.21875
- basis_grad: bfloat16 [3072, 3072], P(None, 'chan'), may hold values from -0.109375 to 0.109375
Outputs:
- act_factor: float32 [768, 768], P('samp', 'chan')
- grad_factor: float32 [3072, 3072], P('samp', 'chan')
- eigen_scales: float32 [3072, 768], P('samp', 'chan')
The draws below stay inside these ranges and needn't reach their ends.
All inputs are finite; a program needn't handle non-finite values.
Results may differ from the reference program's by a relative error of at most 0.0011.
Values may be sent and summed in bfloat16 or wider, within the bound.
No kernel may reach another device: no remote copies, remote signals or barrier semaphores. Data moves between devices by JAX's collectives and lax.ppermute only.
A program may use at most 128 MiB of HBM per device.

```python
import jax
import jax.numpy as jnp
from jax import lax

C = 768
F = 3072
HW = 784
IMAGES = 64
ROWS = 50176


def strengthened(result, rng, source, target, blocks, factor):
    owner, partner = [(jnp.arange(result.shape[axis_at]) // (result.shape[axis_at] // blocks)).reshape([-1 if axis == axis_at else 1 for axis in range(result.ndim)]) for axis_at in (source, target)]
    chosen = jax.random.permutation(rng, blocks)[partner]
    strong = (owner == chosen) | (owner == (partner + blocks // 2) % blocks)
    return jnp.where(strong, factor * result, result)


def block_levels(key, extent, split, low, largest):
    loudness, own = 1.0, jax.random.fold_in(key, 6)
    for dim, shards_of in split:
        steps = jnp.exp(jax.random.uniform(jax.random.fold_in(own, dim), (shards_of,), jnp.float32, low / len(split), largest / len(split)))
        loudness = loudness * jnp.repeat(steps, extent[dim] // shards_of).reshape([-1 if axis == dim else 1 for axis in range(len(extent))])
    return loudness


def noise(own_key, shape, width, limit, cuts=(), held_as=jnp.bfloat16):
    level = block_levels(own_key, shape, cuts, -0.22, 0.18) if cuts else 1.0
    result = jax.random.normal(own_key, shape, jnp.float32) * width * level
    return jnp.minimum(jnp.maximum(result, -limit), limit).astype(held_as)


def gaussian_with(key, dims, spread, bound, cuts, heavy, dtype=jnp.bfloat16):
    drawn = spread * jax.random.normal(key, dims, jnp.float32)
    if cuts:
        drawn = drawn * block_levels(key, dims, cuts, -0.22, 0.18)
    return jnp.clip(strengthened(drawn, jax.random.fold_in(key, 3), *heavy), -bound, bound).astype(dtype)


def setup_inputs(seed: int = 0) -> dict:
    key_list = jax.random.split(jax.random.key(seed), 5)
    return {
        "activations": gaussian_with(key_list[0], (ROWS, C), 1.0, 16.0, ((0, 64), (1, 4)), (0, 1, 64, 4.0)),
        "gradients": gaussian_with(key_list[1], (ROWS, F), 1.0, 16.0, ((0, 64), (1, 4)), (0, 1, 64, 4.0)),
        "basis_act": noise(key_list[2], (C, C), C ** -0.5, 0.21875, ((1, 4),)),
        "basis_grad": noise(key_list[3], (F, F), F ** -0.5, 0.109375, ((1, 4),)),
    }


def crossed(left, right):
    return lax.dot_general(left, right, (((0,), (0,)), ((), ())), preferred_element_type=jnp.float32)


def reference(activations, gradients, basis_act, basis_grad):
    inverse = 1.0 / ROWS
    act_factor = crossed(activations, activations) * inverse
    grad_factor = crossed(gradients, gradients) * inverse
    proj_act = jnp.dot(activations, basis_act, preferred_element_type=jnp.float32).astype(jnp.bfloat16)
    proj_grad = jnp.dot(gradients, basis_grad, preferred_element_type=jnp.float32).astype(jnp.bfloat16)
    act_images = proj_act.reshape(IMAGES, HW, C)
    grad_images = proj_grad.reshape(IMAGES, HW, F)

    def accumulate(carry, pieces):
        per_image = crossed(pieces[1], pieces[0])
        return carry + per_image * per_image, None

    total, unused = lax.scan(accumulate, jnp.zeros((F, C), jnp.float32), (act_images, grad_images))
    eigen_scales = total * (1.0 / (IMAGES * HW))
    return act_factor, grad_factor, eigen_scales
```

```python
import functools

import jax
import jax.numpy as jnp
from jax import lax
from jax.experimental import pallas as pl
from jax.experimental.pallas import tpu as pltpu
from jax.sharding import Mesh, PartitionSpec as P

AXES = ("z", "yl", "x", "yh", "core")
SIZES = (8, 2, 4, 2, 2)
SAMP = ("z", "yl", "x")
CHAN = ("yh", "core")
HW = 784
ROWS = 50176
BLOCK = 768
TILE = 48
PAD = 16
f32, bf16 = jnp.float32, jnp.bfloat16
VMEM = pl.BlockSpec(memory_space=pltpu.VMEM)
SMEM = pl.BlockSpec(memory_space=pltpu.SMEM)
PARAMS = pltpu.CompilerParams(vmem_limit_bytes=48 << 20)


def crossed(left, right):
    return lax.dot_general(
        left, right, (((0,), (0,)), ((), ())), preferred_element_type=f32
    )


def exponent_of(peak):
    e = jnp.floor(jnp.log2(jnp.maximum(peak, 1e-30))) + 1.0
    return jnp.clip(e, -100.0, 100.0)


def coded(value):
    second = value * value
    fourth = second * second
    eighth = fourth * fourth
    return jnp.where(value < 0, -eighth, eighth).astype(bf16)


def decoded(code):
    wide = code.astype(f32)
    root = jnp.exp(0.125 * jnp.log(jnp.maximum(jnp.abs(wide), 1e-37)))
    return jnp.where(wide < 0, -root, root)


def scale_of(e):
    return jnp.exp2(14.0 - e)


def unscale_of(ref, index, row):
    e = ref[index + (pl.ds(row, PAD), pl.ds(0, 128))].astype(f32)[0:1, 0:1]
    return jnp.exp2(e - 14.0)


def peak_of(value, peak):
    return jnp.maximum(peak, jnp.max(jnp.abs(value), axis=(0, 1), keepdims=True))


def put_exponent(ref, index, row, e, width):
    ref[index + (pl.ds(row, PAD), slice(None))] = jnp.broadcast_to(e, (PAD, width)).astype(bf16)


def write_messages(outs, p, x, slots, e):
    scale = scale_of(e)
    for d, out in enumerate(outs):
        to = lax.rem(x + d, 4)
        for b, slot in enumerate(slots):
            for hy in range(4):
                src = pl.multiple_of((hy * 4 + to) * TILE, TILE)
                dst = pl.multiple_of(slot * (4 * TILE) + hy * TILE, TILE)
                out[pl.ds(dst, TILE), :] = coded(p[b, pl.ds(src, TILE), :] * scale)
        put_exponent(out, (), len(slots) * 4 * TILE, e, BLOCK)


def cov_kernel(idx, own, same, other, o0, o1, o2, o3, p):
    x, core = idx[2], idx[4]
    peak = jnp.zeros((1, 1), f32)
    for b, rows in enumerate((same, other)):
        for c in range(3):
            cols = slice(c * 256, (c + 1) * 256)
            tile = crossed(rows[...], own[:, cols]) * (1.0 / ROWS)
            p[b, :, cols] = tile
            peak = peak_of(tile, peak)
    write_messages((o0, o1, o2, o3), p, x, (core, 1 - core), exponent_of(peak))


def messages_of_cov(idx, own, same, other):
    msg = jax.ShapeDtypeStruct((8 * TILE + PAD, BLOCK), bf16)
    return pl.pallas_call(
        cov_kernel,
        out_shape=[msg] * 4,
        in_specs=[SMEM, VMEM, VMEM, VMEM],
        out_specs=[VMEM] * 4,
        scratch_shapes=[pltpu.VMEM((2, BLOCK, BLOCK), f32)],
        compiler_params=PARAMS,
        name="cov",
    )(idx, own, same, other)


def scales_kernel(idx, pg, pa, o0, o1, o2, o3, p):
    x = idx[2]
    peak = jnp.zeros((1, 1), f32)
    for c in range(3):
        cols = slice(c * 256, (c + 1) * 256)
        tile = crossed(pg[...], pa[:, cols])
        tile = tile * tile * (1.0 / ROWS)
        p[0, :, cols] = tile
        peak = peak_of(tile, peak)
    write_messages((o0, o1, o2, o3), p, x, (0,), exponent_of(peak))


def messages_of_scales(idx, pg, pa):
    msg = jax.ShapeDtypeStruct((4 * TILE + PAD, BLOCK), bf16)
    return pl.pallas_call(
        scales_kernel,
        out_shape=[msg] * 4,
        in_specs=[SMEM, VMEM, VMEM],
        out_specs=[VMEM] * 4,
        scratch_shapes=[pltpu.VMEM((1, BLOCK, BLOCK), f32)],
        compiler_params=PARAMS,
        name="scales",
    )(idx, pg, pa)


def sum_x_kernel(blocks, idx, m0, m1, m2, m3, send, keep, held):
    yl = idx[1]
    row = blocks * 2 * TILE
    factors = [unscale_of(m, (), row) for m in (m0, m1, m2, m3)]

    def total(b, y):
        rows = pl.ds(pl.multiple_of((b * 2 + y) * TILE, TILE), TILE)
        parts = [decoded(m[rows, :]) * u for m, u in zip((m0, m1, m2, m3), factors)]
        return (parts[0] + parts[1]) + (parts[2] + parts[3])

    peak = jnp.zeros((1, 1), f32)
    for b in range(blocks):
        keep[b * TILE : (b + 1) * TILE, :] = total(b, yl)
        out = total(b, 1 - yl)
        held[b * TILE : (b + 1) * TILE, :] = out
        peak = peak_of(out, peak)
    e = exponent_of(peak)
    scale = scale_of(e)
    for b in range(blocks):
        rows = slice(b * TILE, (b + 1) * TILE)
        send[rows, :] = coded(held[rows, :] * scale)
    put_exponent(send, (), blocks * TILE, e, BLOCK)


def sum_x(idx, blocks, messages):
    return pl.pallas_call(
        functools.partial(sum_x_kernel, blocks),
        out_shape=[
            jax.ShapeDtypeStruct((blocks * TILE + PAD, BLOCK), bf16),
            jax.ShapeDtypeStruct((blocks * TILE, BLOCK), f32),
        ],
        in_specs=[SMEM] + [VMEM] * 4,
        out_specs=[VMEM] * 2,
        scratch_shapes=[pltpu.VMEM((blocks * TILE, BLOCK), f32)],
        compiler_params=PARAMS,
        name="sum_x",
    )(idx, *messages)


def sum_y_cov_kernel(idx, keep_a, got_a, keep_b, got_b, out, held):
    yh = idx[3]
    peak = jnp.zeros((1, 1), f32)
    for keep, got, half in ((keep_a, got_a, yh), (keep_b, got_b, 1 - yh)):
        unscale = unscale_of(got, (), 4 * TILE)
        for b in range(4):
            rows = slice(b * TILE, (b + 1) * TILE)
            tile = keep[rows, :] + decoded(got[rows, :]) * unscale
            held[half * 4 + b] = tile
            peak = peak_of(tile, peak)
    e = exponent_of(peak)
    scale = scale_of(e)
    for z in range(8):
        out[z, 0:TILE, :] = coded(held[z] * scale)
        put_exponent(out, (z,), TILE, e, BLOCK)


def sum_y_cov(idx, keep_a, got_a, keep_b, got_b):
    return pl.pallas_call(
        sum_y_cov_kernel,
        out_shape=jax.ShapeDtypeStruct((8, TILE + PAD, BLOCK), bf16),
        in_specs=[SMEM] + [VMEM] * 4,
        out_specs=VMEM,
        scratch_shapes=[pltpu.VMEM((8, TILE, BLOCK), f32)],
        compiler_params=PARAMS,
        name="sum_y_cov",
    )(idx, keep_a, got_a, keep_b, got_b)


def sum_y_scales_kernel(keep, got, out):
    unscale = unscale_of(got, (), 2 * TILE)
    tiles, peak = [], jnp.zeros((1, 1), f32)
    for h in range(2):
        rows = slice(h * TILE, (h + 1) * TILE)
        tiles.append(keep[rows, :] + decoded(got[rows, :]) * unscale)
        peak = peak_of(tiles[-1], peak)
    e = exponent_of(peak)
    scale = scale_of(e)
    for h in range(2):
        for j in range(4):
            out[h * 4 + j, 0:TILE, :] = coded(tiles[h][:, j * 192 : (j + 1) * 192] * scale)
            put_exponent(out, (h * 4 + j,), TILE, e, 192)


def sum_y_scales(keep, got):
    return pl.pallas_call(
        sum_y_scales_kernel,
        out_shape=jax.ShapeDtypeStruct((8, TILE + PAD, 192), bf16),
        in_specs=[VMEM] * 2,
        out_specs=VMEM,
        compiler_params=PARAMS,
        name="sum_y_scales",
    )(keep, got)


def sum_z_kernel(m, out):
    total = jnp.zeros(out.shape, f32)
    for z in range(8):
        total = total + decoded(m[z, 0:TILE, :]) * unscale_of(m, (z,), TILE)
    out[...] = total


def sum_z(messages):
    return pl.pallas_call(
        sum_z_kernel,
        out_shape=jax.ShapeDtypeStruct((TILE, messages.shape[2]), f32),
        in_specs=[VMEM],
        out_specs=VMEM,
        compiler_params=PARAMS,
        name="sum_z",
    )(messages)


def swap(value, axis):
    return lax.ppermute(value, axis, [(0, 1), (1, 0)])


def along_x(messages):
    return [messages[0]] + [
        lax.ppermute(messages[d], "x", [(i, (i + d) % 4) for i in range(4)]) for d in (1, 2, 3)
    ]


def final_places():
    pairs = []
    for z in range(8):
        for k in range(4):
            pairs.append((z * 4 + k, (2 * k + z // 4) * 4 + z % 4))
    return pairs


def on_device(activations, gradients, basis_act, basis_grad):
    z, yl, x, yh, core = [lax.axis_index(a) for a in AXES]
    idx = jnp.stack([z, yl, x, yh, core]).astype(jnp.int32)
    chan = yh * 2 + core
    own, other, far, far_other = chan, chan ^ 1, chan ^ 2, chan ^ 3

    both = jnp.concatenate([activations, basis_act], axis=0)
    both_far = swap(both, "yh")
    grad_far = swap(gradients, "yh")
    grad_other = swap(gradients, "core")
    both_other = swap(both, "core")
    msg_a = messages_of_cov(idx, gradients, gradients, grad_other)
    got_a = along_x(msg_a)
    both_far_other = swap(both_far, "core")
    grad_far_other = swap(grad_far, "core")

    def in_order(a, b, c, d):
        low = jnp.where(core == 0, jnp.concatenate([a, b], 1), jnp.concatenate([b, a], 1))
        high = jnp.where(core == 0, jnp.concatenate([c, d], 1), jnp.concatenate([d, c], 1))
        return jnp.where(yh == 0, jnp.concatenate([low, high], 1), jnp.concatenate([high, low], 1))

    both_all = in_order(both, both_other, both_far, both_far_other)
    act_all, basis_all = both_all[:HW], both_all[HW:]
    act_part = crossed(act_all, activations) * (1.0 / ROWS)
    act_got = lax.all_to_all(act_part.reshape(64, 12, 192), SAMP, 0, 0)
    act_factor = jnp.sum(act_got, axis=0)
    proj_act = jnp.dot(act_all, basis_all, preferred_element_type=f32).astype(bf16)

    def rows_of(block):
        return lax.dynamic_slice_in_dim(basis_grad, block * BLOCK, BLOCK, 0)

    proj = jnp.dot(gradients, rows_of(own), preferred_element_type=f32)
    proj = proj + jnp.dot(grad_other, rows_of(other), preferred_element_type=f32)
    keep_a_send, keep_a = sum_x(idx, 4, got_a)

    proj = proj + jnp.dot(grad_far, rows_of(far), preferred_element_type=f32)
    proj = proj + jnp.dot(grad_far_other, rows_of(far_other), preferred_element_type=f32)
    proj_grad = proj.astype(bf16)

    got_e = along_x(messages_of_scales(idx, proj_grad, proj_act))
    got_b = along_x(messages_of_cov(idx, gradients, grad_far, grad_far_other))

    send_e, keep_e = sum_x(idx, 2, got_e)
    y_e = swap(send_e, "yl")
    z_e = lax.all_to_all(sum_y_scales(keep_e, y_e), "z", 0, 0)
    eigen_scales = lax.ppermute(sum_z(z_e), ("z", "yh", "core"), final_places())

    y_a = swap(keep_a_send, "yl")
    send_b, keep_b = sum_x(idx, 4, got_b)
    y_b = swap(send_b, "yl")
    z_cov = lax.all_to_all(sum_y_cov(idx, keep_a, y_a, keep_b, y_b), "z", 0, 0)
    grad_factor = sum_z(z_cov)
    return act_factor, grad_factor, eigen_scales


def solution(mesh):
    fine = Mesh(mesh.devices.reshape(SIZES), AXES)
    return jax.shard_map(
        on_device,
        mesh=fine,
        in_specs=(P(SAMP, CHAN), P(SAMP, CHAN), P(None, CHAN), P(None, CHAN)),
        out_specs=(P(SAMP, CHAN), P(SAMP, CHAN), P(SAMP, CHAN)),
        check_vma=False,
    )
```

```python
import functools

import jax
import jax.numpy as jnp
from jax import lax
from jax.experimental import pallas as pl
from jax.experimental.pallas import tpu as pltpu
from jax.sharding import Mesh, PartitionSpec as P

AXES = ("z", "yl", "x", "yh", "core")
SIZES = (8, 2, 4, 2, 2)
SAMP = ("z", "yl", "x")
CHAN = ("yh", "core")
HW = 784
ROWS = 50176
BLOCK = 768
TILE = 48
HALF = 24
PAD = 16
QUARTER = 192
f32, bf16 = jnp.float32, jnp.bfloat16
VMEM = pl.BlockSpec(memory_space=pltpu.VMEM)
SMEM = pl.BlockSpec(memory_space=pltpu.SMEM)
PARAMS = pltpu.CompilerParams(vmem_limit_bytes=48 << 20)


def crossed(left, right):
    return lax.dot_general(
        left, right, (((0,), (0,)), ((), ())), preferred_element_type=f32
    )


def exponent_of(peak):
    e = jnp.floor(jnp.log2(jnp.maximum(peak, 1e-30))) + 1.0
    return jnp.clip(e, -100.0, 100.0)


def coded(value):
    second = value * value
    fourth = second * second
    eighth = fourth * fourth
    return jnp.where(value < 0, -eighth, eighth)


def decoded(code):
    wide = code.astype(f32)
    root = jnp.exp(0.125 * jnp.log(jnp.maximum(jnp.abs(wide), 1e-37)))
    return jnp.where(wide < 0, -root, root)


def scale_of(e):
    return jnp.exp2(14.0 - e)


def unscale_of(rows):
    return jnp.exp2(rows[0:1, 0:1].astype(f32) - 14.0)


def peak_of(value, peak):
    return jnp.maximum(peak, jnp.max(jnp.abs(value), axis=(0, 1), keepdims=True))


def spread(e, rows, width):
    return jnp.broadcast_to(e, (rows, width))


def call(kernel, name, out_shape, in_specs, scratch=(), flops=0, size=0):
    return pl.pallas_call(
        kernel,
        out_shape=out_shape,
        in_specs=in_specs,
        out_specs=jax.tree.map(lambda _: VMEM, out_shape),
        scratch_shapes=list(scratch),
        compiler_params=PARAMS,
        cost_estimate=pl.CostEstimate(flops=1, bytes_accessed=1, transcendentals=0),
        name=name,
    )


def shape(rows, columns=BLOCK, dtype=bf16):
    return jax.ShapeDtypeStruct((rows, columns), dtype)


def factor_kernel(idx, own, same, other, o0, o1, o2, o3, p):
    x, core = idx[2], idx[4]
    peak = jnp.zeros((1, 1), f32)
    for b, rows in enumerate((same, other)):
        for c in range(3):
            cols = slice(c * 256, (c + 1) * 256)
            tile = crossed(rows[...], own[:, cols]) * (1.0 / ROWS)
            p[b, :, cols] = tile
            peak = peak_of(tile, peak)
    e = exponent_of(peak)
    scale = scale_of(e)
    for d, out in enumerate((o0, o1, o2, o3)):
        to = lax.rem(x + d, 4)
        for b, slot in enumerate((core, 1 - core)):
            for hy in range(4):
                src = pl.multiple_of((hy * 4 + to) * TILE, TILE)
                dst = pl.multiple_of((slot * 4 + hy) * TILE, TILE)
                out[pl.ds(dst, TILE), :] = coded(p[b, pl.ds(src, TILE), :] * scale).astype(bf16)
        out[8 * TILE :, :] = spread(e, PAD, BLOCK).astype(bf16)


def factor_messages(idx, own, same, other):
    return call(
        factor_kernel,
        "factor",
        [shape(8 * TILE + PAD)] * 4,
        [SMEM] + [VMEM] * 3,
        [pltpu.VMEM((2, BLOCK, BLOCK), f32)],
    )(idx, own, same, other)


def factor_sum_x_kernel(idx, m0, m1, m2, m3, send, keep, held):
    yl = idx[1]
    factors = [unscale_of(m[8 * TILE :, 0:128]) for m in (m0, m1, m2, m3)]

    def total(b, y):
        rows = pl.ds(pl.multiple_of((b * 2 + y) * TILE, TILE), TILE)
        parts = [decoded(m[rows, :]) * u for m, u in zip((m0, m1, m2, m3), factors)]
        return (parts[0] + parts[1]) + (parts[2] + parts[3])

    peak = jnp.zeros((1, 1), f32)
    for b in range(4):
        keep[b * TILE : (b + 1) * TILE, :] = total(b, yl)
        out = total(b, 1 - yl)
        held[b * TILE : (b + 1) * TILE, :] = out
        peak = peak_of(out, peak)
    e = exponent_of(peak)
    send[0 : 4 * TILE, :] = coded(held[...] * scale_of(e)).astype(bf16)
    send[4 * TILE :, :] = spread(e, PAD, BLOCK).astype(bf16)


def factor_sum_x(idx, messages):
    return call(
        factor_sum_x_kernel,
        "factor_sum_x",
        [shape(4 * TILE + PAD), shape(4 * TILE, dtype=f32)],
        [SMEM] + [VMEM] * 4,
        [pltpu.VMEM((4 * TILE, BLOCK), f32)],
    )(idx, *messages)


def factor_sum_y_kernel(idx, keep_a, got_a, keep_b, got_b, out, held):
    yh = idx[3]
    peak = jnp.zeros((1, 1), f32)
    for keep, got, half in ((keep_a, got_a, yh), (keep_b, got_b, 1 - yh)):
        unscale = unscale_of(got[4 * TILE :, 0:128])
        for b in range(4):
            rows = slice(b * TILE, (b + 1) * TILE)
            tile = keep[rows, :] + decoded(got[rows, :]) * unscale
            held[half * 4 + b] = tile
            peak = peak_of(tile, peak)
    e = exponent_of(peak)
    scale = scale_of(e)
    for z in range(8):
        out[z, 0:TILE, :] = coded(held[z] * scale).astype(bf16)
        out[z, TILE:, :] = spread(e, PAD, BLOCK).astype(bf16)


def factor_sum_y(idx, keep_a, got_a, keep_b, got_b):
    return call(
        factor_sum_y_kernel,
        "factor_sum_y",
        jax.ShapeDtypeStruct((8, TILE + PAD, BLOCK), bf16),
        [SMEM] + [VMEM] * 4,
        [pltpu.VMEM((8, TILE, BLOCK), f32)],
    )(idx, keep_a, got_a, keep_b, got_b)


def factor_sum_z_kernel(m, out):
    total = jnp.zeros(out.shape, f32)
    for z in range(8):
        total = total + decoded(m[z, 0:TILE, :]) * unscale_of(m[z, TILE:, 0:128])
    out[...] = total


def factor_sum_z(messages):
    return call(factor_sum_z_kernel, "factor_sum_z", shape(TILE, dtype=f32), [VMEM])(messages)


def proj_kernel(first, idx, a, b, basis, *rest):
    before, out = (None, rest[0]) if len(rest) == 1 else rest
    chan = idx[3] * 2 + idx[4]
    width = a.shape[1]
    flip, offset = first
    for c in range(3):
        cols = slice(c * 256, (c + 1) * 256)
        total = None if before is None else before[:, cols]
        for n, part in enumerate((a, b)):
            start = pl.multiple_of((chan ^ (flip + n)) * BLOCK + offset, 128)
            term = jnp.dot(part[...], basis[pl.ds(start, width), cols], preferred_element_type=f32)
            total = term if total is None else total + term
        out[:, cols] = total.astype(out.dtype)


def project(idx, first, a, b, basis, before, dtype):
    operands = (idx, a, b, basis) + (() if before is None else (before,))
    return call(
        functools.partial(proj_kernel, first),
        "project",
        shape(HW, dtype=dtype),
        [SMEM] + [VMEM] * (len(operands) - 1),
        flops=4 * HW * a.shape[1] * BLOCK,
        size=8 << 20,
    )(*operands)


def beside_kernel(act, basis, out):
    out[:, 0:QUARTER] = act[...]
    out[0:BLOCK, QUARTER:] = basis[...]
    out[BLOCK:, QUARTER:] = jnp.zeros((HW - BLOCK, QUARTER), bf16)


def side_by_side(act, basis):
    return call(beside_kernel, "beside", shape(HW, 2 * QUARTER), [VMEM] * 2)(act, basis)


def act_kernel(idx, b0, b1, b2, b3, pa, act, basis, part):
    chan = idx[3] * 2 + idx[4]
    blocks = (b0, b1, b2, b3)
    for m, block in enumerate(blocks):
        cols = slice(m * QUARTER, (m + 1) * QUARTER)
        basis[:, cols] = block[0:BLOCK, QUARTER:]
        part[cols, :] = crossed(block[:, 0:QUARTER], b0[:, 0:QUARTER]) * (1.0 / ROWS)
    for c in range(3):
        cols = slice(c * 256, (c + 1) * 256)
        total = None
        for m, block in enumerate(blocks):
            start = pl.multiple_of((chan ^ m) * QUARTER, 64)
            term = jnp.dot(
                block[:, 0:QUARTER],
                basis[pl.ds(start, QUARTER), cols],
                preferred_element_type=f32,
            )
            total = term if total is None else total + term
        pa[:, cols] = total.astype(bf16)
    for to in range(4):
        for y in range(2):
            for m in range(4):
                for h in range(2):
                    src = m * QUARTER + (h * 8 + y * 4 + to) * 12
                    dst = y * HALF + h * 12
                    act[to, dst : dst + 12, m * QUARTER : (m + 1) * QUARTER] = part[src : src + 12, :]


def act_parts(idx, blocks):
    return call(
        act_kernel,
        "act",
        [shape(HW), jax.ShapeDtypeStruct((4, 2 * HALF, BLOCK), f32)],
        [SMEM] + [VMEM] * 4,
        [pltpu.VMEM((BLOCK, BLOCK), bf16), pltpu.VMEM((BLOCK, QUARTER), f32)],
        flops=2 * HW * BLOCK * 960,
        size=4 << 20,
    )(idx, *blocks)


def scales_kernel(idx, pg, pa, act, o0, o1, o2, o3, p):
    x = idx[2]
    peak = jnp.zeros((1, 1), f32)
    for c in range(3):
        cols = slice(c * 256, (c + 1) * 256)
        tile = crossed(pg[...], pa[:, cols])
        tile = tile * tile * (1.0 / ROWS)
        p[:, cols] = tile
        peak = peak_of(tile, peak)
    e = exponent_of(peak)
    scale = scale_of(e)
    act_peak = jnp.zeros((1, 1), f32)
    for to in range(4):
        act_peak = peak_of(act[to], act_peak)
    act_e = exponent_of(act_peak)
    act_scale = scale_of(act_e)
    for d, out in enumerate((o0, o1, o2, o3)):
        to = lax.rem(x + d, 4)
        for hy in range(4):
            src = pl.multiple_of((hy * 4 + to) * TILE, TILE)
            out[hy * TILE : (hy + 1) * TILE, :] = coded(p[pl.ds(src, TILE), :] * scale).astype(bf16)
        out[4 * TILE : 5 * TILE, :] = coded(act[to] * act_scale).astype(bf16)
        out[5 * TILE :, :] = jnp.concatenate(
            [spread(e, 8, BLOCK), spread(act_e, 8, BLOCK)], axis=0
        ).astype(bf16)


def scales_messages(idx, pg, pa, act):
    return call(
        scales_kernel,
        "scales",
        [shape(5 * TILE + PAD)] * 4,
        [SMEM] + [VMEM] * 3,
        [pltpu.VMEM((BLOCK, BLOCK), f32)],
        flops=2 * HW * BLOCK * BLOCK,
        size=4 << 20,
    )(idx, pg, pa, act)


def scales_sum_x_kernel(idx, m0, m1, m2, m3, send, keep, keep_act, held, held_act):
    yl = idx[1]
    messages = (m0, m1, m2, m3)
    ends = [m[5 * TILE :, 0:128].astype(f32) for m in messages]
    factors = [unscale_of(end) for end in ends]
    act_factors = [unscale_of(end[8:, :]) for end in ends]

    def total(h, y):
        rows = pl.ds(pl.multiple_of((h * 2 + y) * TILE, TILE), TILE)
        parts = [decoded(m[rows, :]) * u for m, u in zip(messages, factors)]
        return (parts[0] + parts[1]) + (parts[2] + parts[3])

    peak = jnp.zeros((1, 1), f32)
    for h in range(2):
        keep[h * TILE : (h + 1) * TILE, :] = total(h, yl)
        out = total(h, 1 - yl)
        held[h * TILE : (h + 1) * TILE, :] = out
        peak = peak_of(out, peak)
    parts = [decoded(m[4 * TILE : 5 * TILE, :]) * u for m, u in zip(messages, act_factors)]
    held_act[...] = (parts[0] + parts[1]) + (parts[2] + parts[3])
    keep_act[...] = held_act[pl.ds(pl.multiple_of(yl * HALF, 8), HALF), :]
    out = held_act[pl.ds(pl.multiple_of((1 - yl) * HALF, 8), HALF), :]
    e = exponent_of(peak)
    act_e = exponent_of(peak_of(out, jnp.zeros((1, 1), f32)))
    send[0 : 2 * TILE, :] = coded(held[...] * scale_of(e)).astype(bf16)
    send[2 * TILE : 2 * TILE + 32, :] = jnp.concatenate(
        [coded(out * scale_of(act_e)), spread(e, 8, BLOCK)], axis=0
    ).astype(bf16)
    send[2 * TILE + 32 :, :] = spread(act_e, PAD, BLOCK).astype(bf16)


def scales_sum_x(idx, messages):
    return call(
        scales_sum_x_kernel,
        "scales_sum_x",
        [shape(2 * TILE + 32 + PAD), shape(2 * TILE, dtype=f32), shape(HALF, dtype=f32)],
        [SMEM] + [VMEM] * 4,
        [pltpu.VMEM((2 * TILE, BLOCK), f32), pltpu.VMEM((2 * HALF, BLOCK), f32)],
        size=2 << 20,
    )(idx, *messages)


def scales_sum_y_kernel(idx, keep, keep_act, got, out):
    chan = idx[3] * 2 + idx[4]
    end = got[2 * TILE : 2 * TILE + 32, :].astype(f32)
    act_end = got[2 * TILE + 32 :, 0:128].astype(f32)
    tile = keep[...] + decoded(got[0 : 2 * TILE, :]) * unscale_of(end[HALF:, :])
    act = keep_act[...] + decoded(end[0:HALF, :]) * unscale_of(act_end)
    e = exponent_of(peak_of(tile, jnp.zeros((1, 1), f32)))
    act_e = exponent_of(peak_of(act, jnp.zeros((1, 1), f32)))
    tile = coded(tile * scale_of(e)).astype(bf16)
    act = coded(act * scale_of(act_e))
    for h in range(2):
        for m in range(4):
            cols = slice(m * QUARTER, (m + 1) * QUARTER)
            out[h * 4 + (chan ^ m), 0:TILE, :] = tile[h * TILE : (h + 1) * TILE, cols]
            out[(chan ^ m) * 2 + h, TILE:, :] = jnp.concatenate(
                [act[h * 12 : (h + 1) * 12, cols], spread(e, 2, QUARTER), spread(act_e, 2, QUARTER)],
                axis=0,
            ).astype(bf16)


def scales_sum_y(idx, keep, keep_act, got):
    return call(
        scales_sum_y_kernel,
        "scales_sum_y",
        jax.ShapeDtypeStruct((8, TILE + 16, QUARTER), bf16),
        [SMEM] + [VMEM] * 3,
        size=1 << 20,
    )(idx, keep, keep_act, got)


def scales_sum_z_kernel(m, out, act):
    total = jnp.zeros((TILE, QUARTER), f32)
    total_act = jnp.zeros((12, QUARTER), f32)
    for z in range(8):
        end = m[z, TILE:, :].astype(f32)
        total = total + decoded(m[z, 0:TILE, :]) * unscale_of(end[12:14, :])
        total_act = total_act + decoded(end[0:12, :]) * unscale_of(end[14:16, :])
    out[...] = total
    act[...] = total_act


def scales_sum_z(messages):
    return call(
        scales_sum_z_kernel,
        "scales_sum_z",
        [shape(TILE, QUARTER, f32), shape(12, QUARTER, f32)],
        [VMEM],
        size=1 << 18,
    )(messages)


def after(value, *earlier):
    return lax.optimization_barrier((value,) + earlier)[0]


def swap(value, axis):
    return lax.ppermute(value, axis, [(0, 1), (1, 0)])


def along_x(messages):
    return [messages[0]] + [
        lax.ppermute(messages[d], "x", [(i, (i + d) % 4) for i in range(4)]) for d in (1, 3, 2)
    ]


def scales_places():
    return [
        (z * 4 + k, (2 * k + z // 4) * 4 + z % 4) for z in range(8) for k in range(4)
    ]


def on_device(activations, gradients, basis_act, basis_grad):
    z, yl, x, yh, core = [lax.axis_index(a) for a in AXES]
    idx = jnp.stack([z, yl, x, yh, core]).astype(jnp.int32)

    grad_far = swap(gradients, "yh")
    grad_other = swap(gradients, "core")
    both = side_by_side(activations, basis_act)
    both_other = swap(both, "core")

    msg_a = factor_messages(idx, gradients, gradients, grad_other)
    got_a = along_x(msg_a)
    proj = project(idx, (0, 0), after(gradients, both_other, *msg_a), grad_other, basis_grad, None, f32)

    grad_far, proj = lax.optimization_barrier((grad_far, proj))
    grad_far_other = swap(after(grad_far, *got_a[1:3]), "core")
    both_far = swap(after(both, grad_far), "yh")
    msg_b = factor_messages(idx, gradients, grad_far, grad_far_other)
    proj, *got_a = lax.optimization_barrier((proj,) + tuple(got_a) + tuple(msg_b))[:5]
    got_b = along_x(msg_b)
    proj_grad = project(idx, (2, 0), grad_far, grad_far_other, basis_grad, proj, bf16)
    both_far_other = swap(after(both_far, proj_grad), "core")

    proj_act, act = act_parts(idx, (both, both_other, both_far, both_far_other))
    msg_e = scales_messages(idx, proj_grad, proj_act, act)
    got_e = along_x(msg_e)

    send_a, keep_a = factor_sum_x(idx, [after(got_a[0], *msg_e)] + list(got_a[1:]))
    y_a = swap(send_a, "yl")
    send_b, keep_b = factor_sum_x(idx, [after(got_b[0], send_a)] + got_b[1:])
    y_b = swap(send_b, "yl")
    to_z = factor_sum_y(idx, keep_a, y_a, keep_b, y_b)
    z_cov = lax.all_to_all(to_z, "z", 0, 0)
    grad_factor = factor_sum_z(z_cov)

    send_e, keep_e, keep_act = scales_sum_x(idx, [after(got_e[0], to_z)] + got_e[1:])
    y_e = swap(send_e, "yl")
    z_e = lax.all_to_all(after(scales_sum_y(idx, keep_e, keep_act, y_e), z_cov), "z", 0, 0)
    scales, act_factor = scales_sum_z(z_e)
    eigen_scales = lax.ppermute(scales, ("z", "yh", "core"), scales_places())
    return act_factor, grad_factor, eigen_scales


def solution(mesh):
    fine = Mesh(mesh.devices.reshape(SIZES), AXES)
    return jax.shard_map(
        on_device,
        mesh=fine,
        in_specs=(P(SAMP, CHAN), P(SAMP, CHAN), P(None, CHAN), P(None, CHAN)),
        out_specs=(P(SAMP, CHAN), P(SAMP, CHAN), P(SAMP, CHAN)),
        check_vma=False,
    )
```

```python
import functools

import jax
import jax.numpy as jnp
from jax import lax
from jax.experimental import pallas as pl
from jax.experimental.pallas import tpu as pltpu
from jax.sharding import Mesh, PartitionSpec as P

AXES = ("z", "yl", "x", "yh", "core")
SIZES = (8, 2, 4, 2, 2)
SAMP = ("z", "yl", "x")
CHAN = ("yh", "core")
HW = 784
ROWS = 50176
BLOCK = 768
TILE = 48
HALF = 24
PAD = 16
QUARTER = 192
f32, bf16 = jnp.float32, jnp.bfloat16
VMEM = pl.BlockSpec(memory_space=pltpu.VMEM)
SMEM = pl.BlockSpec(memory_space=pltpu.SMEM)
PARAMS = pltpu.CompilerParams(vmem_limit_bytes=48 << 20)


def crossed(left, right):
    return lax.dot_general(
        left, right, (((0,), (0,)), ((), ())), preferred_element_type=f32
    )


def exponent_of(peak):
    e = jnp.floor(jnp.log2(jnp.maximum(peak, 1e-30))) + 1.0
    return jnp.clip(e, -100.0, 100.0)


def coded(value):
    second = value * value
    fourth = second * second
    eighth = fourth * fourth
    return jnp.where(value < 0, -eighth, eighth)


def decoded(code):
    wide = code.astype(f32)
    root = jnp.exp(0.125 * jnp.log(jnp.maximum(jnp.abs(wide), 1e-37)))
    return jnp.where(wide < 0, -root, root)


def scale_of(e):
    return jnp.exp2(14.0 - e)


def unscale_of(rows):
    return jnp.exp2(rows[0:1, 0:1].astype(f32) - 14.0)


def peak_of(value, peak):
    return jnp.maximum(peak, jnp.max(jnp.abs(value), axis=(0, 1), keepdims=True))


def spread(e, rows, width):
    return jnp.broadcast_to(e, (rows, width))


def call(kernel, name, out_shape, in_specs, scratch=(), flops=0, size=0):
    return pl.pallas_call(
        kernel,
        out_shape=out_shape,
        in_specs=in_specs,
        out_specs=jax.tree.map(lambda _: VMEM, out_shape),
        scratch_shapes=list(scratch),
        compiler_params=PARAMS,
        cost_estimate=pl.CostEstimate(flops=1, bytes_accessed=1, transcendentals=0),
        name=name,
    )


def shape(rows, columns=BLOCK, dtype=bf16):
    return jax.ShapeDtypeStruct((rows, columns), dtype)


def factor_kernel(idx, own, same, other, o0, o1, o2, o3, p):
    x, core = idx[2], idx[4]
    peak = jnp.zeros((1, 1), f32)
    for b, rows in enumerate((same, other)):
        for c in range(3):
            cols = slice(c * 256, (c + 1) * 256)
            tile = crossed(rows[...], own[:, cols]) * (1.0 / ROWS)
            p[b, :, cols] = tile
            peak = peak_of(tile, peak)
    e = exponent_of(peak)
    scale = scale_of(e)
    for d, out in enumerate((o0, o1, o2, o3)):
        to = lax.rem(x + d, 4)
        for b, slot in enumerate((core, 1 - core)):
            for hy in range(4):
                src = pl.multiple_of((hy * 4 + to) * TILE, TILE)
                dst = pl.multiple_of((slot * 4 + hy) * TILE, TILE)
                out[pl.ds(dst, TILE), :] = coded(p[b, pl.ds(src, TILE), :] * scale).astype(bf16)
        out[8 * TILE :, :] = spread(e, PAD, BLOCK).astype(bf16)


def factor_messages(idx, own, same, other):
    return call(
        factor_kernel,
        "factor",
        [shape(8 * TILE + PAD)] * 4,
        [SMEM] + [VMEM] * 3,
        [pltpu.VMEM((2, BLOCK, BLOCK), f32)],
    )(idx, own, same, other)


def factor_sum_x_kernel(idx, m0, m1, m2, m3, send, keep, held):
    yl = idx[1]
    factors = [unscale_of(m[8 * TILE :, 0:128]) for m in (m0, m1, m2, m3)]

    def total(b, y):
        rows = pl.ds(pl.multiple_of((b * 2 + y) * TILE, TILE), TILE)
        parts = [decoded(m[rows, :]) * u for m, u in zip((m0, m1, m2, m3), factors)]
        return (parts[0] + parts[1]) + (parts[2] + parts[3])

    peak = jnp.zeros((1, 1), f32)
    for b in range(4):
        keep[b * TILE : (b + 1) * TILE, :] = total(b, yl)
        out = total(b, 1 - yl)
        held[b * TILE : (b + 1) * TILE, :] = out
        peak = peak_of(out, peak)
    e = exponent_of(peak)
    send[0 : 4 * TILE, :] = coded(held[...] * scale_of(e)).astype(bf16)
    send[4 * TILE :, :] = spread(e, PAD, BLOCK).astype(bf16)


def factor_sum_x(idx, messages):
    return call(
        factor_sum_x_kernel,
        "factor_sum_x",
        [shape(4 * TILE + PAD), shape(4 * TILE, dtype=f32)],
        [SMEM] + [VMEM] * 4,
        [pltpu.VMEM((4 * TILE, BLOCK), f32)],
    )(idx, *messages)


def factor_sum_y_kernel(idx, keep_a, got_a, keep_b, got_b, out, held):
    yh = idx[3]
    peak = jnp.zeros((1, 1), f32)
    for keep, got, half in ((keep_a, got_a, yh), (keep_b, got_b, 1 - yh)):
        unscale = unscale_of(got[4 * TILE :, 0:128])
        for b in range(4):
            rows = slice(b * TILE, (b + 1) * TILE)
            tile = keep[rows, :] + decoded(got[rows, :]) * unscale
            held[half * 4 + b] = tile
            peak = peak_of(tile, peak)
    e = exponent_of(peak)
    scale = scale_of(e)
    for z in range(8):
        out[z, 0:TILE, :] = coded(held[z] * scale).astype(bf16)
        out[z, TILE:, :] = spread(e, PAD, BLOCK).astype(bf16)


def factor_sum_y(idx, keep_a, got_a, keep_b, got_b):
    return call(
        factor_sum_y_kernel,
        "factor_sum_y",
        jax.ShapeDtypeStruct((8, TILE + PAD, BLOCK), bf16),
        [SMEM] + [VMEM] * 4,
        [pltpu.VMEM((8, TILE, BLOCK), f32)],
    )(idx, keep_a, got_a, keep_b, got_b)


def factor_sum_z_kernel(m, out):
    total = jnp.zeros(out.shape, f32)
    for z in range(8):
        total = total + decoded(m[z, 0:TILE, :]) * unscale_of(m[z, TILE:, 0:128])
    out[...] = total


def factor_sum_z(messages):
    return call(factor_sum_z_kernel, "factor_sum_z", shape(TILE, dtype=f32), [VMEM])(messages)


def factor_parts(own, same, other, p):
    peak = jnp.zeros((1, 1), f32)
    for b, rows in enumerate((same, other)):
        for c in range(3):
            cols = slice(c * 256, (c + 1) * 256)
            tile = crossed(rows[...], own[:, cols]) * (1.0 / ROWS)
            p[b, :, cols] = tile
            peak = peak_of(tile, peak)
    return exponent_of(peak)


def near_kernel(idx, own, same, other, out, p):
    core = idx[4]
    e = factor_parts(own, same, other, p)
    scale = scale_of(e)
    for b, slot in enumerate((core, 1 - core)):
        for hyx in range(16):
            dst = pl.multiple_of((slot * 4 + hyx // 4) * TILE, TILE)
            src = slice(hyx * TILE, (hyx + 1) * TILE)
            out[hyx % 4, pl.ds(dst, TILE), :] = coded(p[b, src, :] * scale).astype(bf16)
    for x in range(4):
        out[x, 8 * TILE :, :] = spread(e, PAD, BLOCK).astype(bf16)


def near_messages(idx, own, same, other):
    return call(
        near_kernel,
        "near",
        jax.ShapeDtypeStruct((4, 8 * TILE + PAD, BLOCK), bf16),
        [SMEM] + [VMEM] * 3,
        [pltpu.VMEM((2, BLOCK, BLOCK), f32)],
    )(idx, own, same, other)


def near_sum_x_kernel(idx, m, send, keep, held):
    yl = idx[1]
    factors = [unscale_of(m[d, 8 * TILE :, 0:128]) for d in range(4)]

    def total(b, y):
        rows = pl.ds(pl.multiple_of((b * 2 + y) * TILE, TILE), TILE)
        parts = [decoded(m[d, rows, :]) * factors[d] for d in range(4)]
        return (parts[0] + parts[1]) + (parts[2] + parts[3])

    peak = jnp.zeros((1, 1), f32)
    for b in range(4):
        keep[b * TILE : (b + 1) * TILE, :] = total(b, yl)
        out = total(b, 1 - yl)
        held[b * TILE : (b + 1) * TILE, :] = out
        peak = peak_of(out, peak)
    e = exponent_of(peak)
    send[0 : 4 * TILE, :] = coded(held[...] * scale_of(e)).astype(bf16)
    send[4 * TILE :, :] = spread(e, PAD, BLOCK).astype(bf16)


def near_sum_x(idx, messages):
    return call(
        near_sum_x_kernel,
        "near_sum_x",
        [shape(4 * TILE + PAD), shape(4 * TILE, dtype=f32)],
        [SMEM, VMEM],
        [pltpu.VMEM((4 * TILE, BLOCK), f32)],
    )(idx, messages)


def proj_kernel(first, idx, a, b, basis, *rest):
    before, out = (None, rest[0]) if len(rest) == 1 else rest
    chan = idx[3] * 2 + idx[4]
    width = a.shape[1]
    flip, offset = first
    for c in range(3):
        cols = slice(c * 256, (c + 1) * 256)
        total = None if before is None else before[:, cols]
        for n, part in enumerate((a, b)):
            start = pl.multiple_of((chan ^ (flip + n)) * BLOCK + offset, 128)
            term = jnp.dot(part[...], basis[pl.ds(start, width), cols], preferred_element_type=f32)
            total = term if total is None else total + term
        out[:, cols] = total.astype(out.dtype)


def project(idx, first, a, b, basis, before, dtype):
    operands = (idx, a, b, basis) + (() if before is None else (before,))
    return call(
        functools.partial(proj_kernel, first),
        "project",
        shape(HW, dtype=dtype),
        [SMEM] + [VMEM] * (len(operands) - 1),
        flops=4 * HW * a.shape[1] * BLOCK,
        size=8 << 20,
    )(*operands)


def beside_kernel(act, basis, out):
    out[:, 0:QUARTER] = act[...]
    out[0:BLOCK, QUARTER:] = basis[...]
    out[BLOCK:, QUARTER:] = jnp.zeros((HW - BLOCK, QUARTER), bf16)


def side_by_side(act, basis):
    return call(beside_kernel, "beside", shape(HW, 2 * QUARTER), [VMEM] * 2)(act, basis)


def act_kernel(idx, b0, b1, b2, b3, pa, act, basis, part):
    chan = idx[3] * 2 + idx[4]
    blocks = (b0, b1, b2, b3)
    for m, block in enumerate(blocks):
        cols = slice(m * QUARTER, (m + 1) * QUARTER)
        basis[:, cols] = block[0:BLOCK, QUARTER:]
        part[cols, :] = crossed(block[:, 0:QUARTER], b0[:, 0:QUARTER]) * (1.0 / ROWS)
    for c in range(3):
        cols = slice(c * 256, (c + 1) * 256)
        total = None
        for m, block in enumerate(blocks):
            start = pl.multiple_of((chan ^ m) * QUARTER, 64)
            term = jnp.dot(
                block[:, 0:QUARTER],
                basis[pl.ds(start, QUARTER), cols],
                preferred_element_type=f32,
            )
            total = term if total is None else total + term
        pa[:, cols] = total.astype(bf16)
    for to in range(4):
        for y in range(2):
            for m in range(4):
                for h in range(2):
                    src = m * QUARTER + (h * 8 + y * 4 + to) * 12
                    dst = y * HALF + h * 12
                    act[to, dst : dst + 12, m * QUARTER : (m + 1) * QUARTER] = part[src : src + 12, :]


def act_parts(idx, blocks):
    return call(
        act_kernel,
        "act",
        [shape(HW), jax.ShapeDtypeStruct((4, 2 * HALF, BLOCK), f32)],
        [SMEM] + [VMEM] * 4,
        [pltpu.VMEM((BLOCK, BLOCK), bf16), pltpu.VMEM((BLOCK, QUARTER), f32)],
        flops=2 * HW * BLOCK * 960,
        size=4 << 20,
    )(idx, *blocks)


def scales_kernel(idx, pg, pa, act, o0, o1, o2, o3, p):
    x = idx[2]
    peak = jnp.zeros((1, 1), f32)
    for c in range(3):
        cols = slice(c * 256, (c + 1) * 256)
        tile = crossed(pg[...], pa[:, cols])
        tile = tile * tile * (1.0 / ROWS)
        p[:, cols] = tile
        peak = peak_of(tile, peak)
    e = exponent_of(peak)
    scale = scale_of(e)
    act_peak = jnp.zeros((1, 1), f32)
    for to in range(4):
        act_peak = peak_of(act[to], act_peak)
    act_e = exponent_of(act_peak)
    act_scale = scale_of(act_e)
    for d, out in enumerate((o0, o1, o2, o3)):
        to = lax.rem(x + d, 4)
        for hy in range(4):
            src = pl.multiple_of((hy * 4 + to) * TILE, TILE)
            out[hy * TILE : (hy + 1) * TILE, :] = coded(p[pl.ds(src, TILE), :] * scale).astype(bf16)
        out[4 * TILE : 5 * TILE, :] = coded(act[to] * act_scale).astype(bf16)
        out[5 * TILE :, :] = jnp.concatenate(
            [spread(e, 8, BLOCK), spread(act_e, 8, BLOCK)], axis=0
        ).astype(bf16)


def scales_messages(idx, pg, pa, act):
    return call(
        scales_kernel,
        "scales",
        [shape(5 * TILE + PAD)] * 4,
        [SMEM] + [VMEM] * 3,
        [pltpu.VMEM((BLOCK, BLOCK), f32)],
        flops=2 * HW * BLOCK * BLOCK,
        size=4 << 20,
    )(idx, pg, pa, act)


def scales_sum_x_kernel(idx, m0, m1, m2, m3, send, keep, keep_act, held, held_act):
    yl = idx[1]
    messages = (m0, m1, m2, m3)
    ends = [m[5 * TILE :, 0:128].astype(f32) for m in messages]
    factors = [unscale_of(end) for end in ends]
    act_factors = [unscale_of(end[8:, :]) for end in ends]

    def total(h, y):
        rows = pl.ds(pl.multiple_of((h * 2 + y) * TILE, TILE), TILE)
        parts = [decoded(m[rows, :]) * u for m, u in zip(messages, factors)]
        return (parts[0] + parts[1]) + (parts[2] + parts[3])

    peak = jnp.zeros((1, 1), f32)
    for h in range(2):
        keep[h * TILE : (h + 1) * TILE, :] = total(h, yl)
        out = total(h, 1 - yl)
        held[h * TILE : (h + 1) * TILE, :] = out
        peak = peak_of(out, peak)
    parts = [decoded(m[4 * TILE : 5 * TILE, :]) * u for m, u in zip(messages, act_factors)]
    held_act[...] = (parts[0] + parts[1]) + (parts[2] + parts[3])
    keep_act[...] = held_act[pl.ds(pl.multiple_of(yl * HALF, 8), HALF), :]
    out = held_act[pl.ds(pl.multiple_of((1 - yl) * HALF, 8), HALF), :]
    e = exponent_of(peak)
    act_e = exponent_of(peak_of(out, jnp.zeros((1, 1), f32)))
    send[0 : 2 * TILE, :] = coded(held[...] * scale_of(e)).astype(bf16)
    send[2 * TILE : 2 * TILE + 32, :] = jnp.concatenate(
        [coded(out * scale_of(act_e)), spread(e, 8, BLOCK)], axis=0
    ).astype(bf16)
    send[2 * TILE + 32 :, :] = spread(act_e, PAD, BLOCK).astype(bf16)


def scales_sum_x(idx, messages):
    return call(
        scales_sum_x_kernel,
        "scales_sum_x",
        [shape(2 * TILE + 32 + PAD), shape(2 * TILE, dtype=f32), shape(HALF, dtype=f32)],
        [SMEM] + [VMEM] * 4,
        [pltpu.VMEM((2 * TILE, BLOCK), f32), pltpu.VMEM((2 * HALF, BLOCK), f32)],
        size=2 << 20,
    )(idx, *messages)


def scales_sum_y_kernel(idx, keep, keep_act, got, out):
    chan = idx[3] * 2 + idx[4]
    end = got[2 * TILE : 2 * TILE + 32, :].astype(f32)
    act_end = got[2 * TILE + 32 :, 0:128].astype(f32)
    tile = keep[...] + decoded(got[0 : 2 * TILE, :]) * unscale_of(end[HALF:, :])
    act = keep_act[...] + decoded(end[0:HALF, :]) * unscale_of(act_end)
    e = exponent_of(peak_of(tile, jnp.zeros((1, 1), f32)))
    act_e = exponent_of(peak_of(act, jnp.zeros((1, 1), f32)))
    tile = coded(tile * scale_of(e)).astype(bf16)
    act = coded(act * scale_of(act_e))
    for h in range(2):
        for m in range(4):
            cols = slice(m * QUARTER, (m + 1) * QUARTER)
            out[h * 4 + (chan ^ m), 0:TILE, :] = tile[h * TILE : (h + 1) * TILE, cols]
            out[(chan ^ m) * 2 + h, TILE:, :] = jnp.concatenate(
                [act[h * 12 : (h + 1) * 12, cols], spread(e, 2, QUARTER), spread(act_e, 2, QUARTER)],
                axis=0,
            ).astype(bf16)


def scales_sum_y(idx, keep, keep_act, got):
    return call(
        scales_sum_y_kernel,
        "scales_sum_y",
        jax.ShapeDtypeStruct((8, TILE + 16, QUARTER), bf16),
        [SMEM] + [VMEM] * 3,
        size=1 << 20,
    )(idx, keep, keep_act, got)


def scales_sum_z_kernel(m, out, act):
    total = jnp.zeros((TILE, QUARTER), f32)
    total_act = jnp.zeros((12, QUARTER), f32)
    for z in range(8):
        end = m[z, TILE:, :].astype(f32)
        total = total + decoded(m[z, 0:TILE, :]) * unscale_of(end[12:14, :])
        total_act = total_act + decoded(end[0:12, :]) * unscale_of(end[14:16, :])
    out[...] = total
    act[...] = total_act


def scales_sum_z(messages):
    return call(
        scales_sum_z_kernel,
        "scales_sum_z",
        [shape(TILE, QUARTER, f32), shape(12, QUARTER, f32)],
        [VMEM],
        size=1 << 18,
    )(messages)


def after(value, *earlier):
    return lax.optimization_barrier((value,) + earlier)[0]


def swap(value, axis):
    return lax.ppermute(value, axis, [(0, 1), (1, 0)])


def along_x(messages):
    return [messages[0]] + [
        lax.ppermute(messages[d], "x", [(i, (i + d) % 4) for i in range(4)]) for d in (1, 3, 2)
    ]


def scales_places():
    return [
        (z * 4 + k, (2 * k + z // 4) * 4 + z % 4) for z in range(8) for k in range(4)
    ]


def on_device(activations, gradients, basis_act, basis_grad):
    z, yl, x, yh, core = [lax.axis_index(a) for a in AXES]
    idx = jnp.stack([z, yl, x, yh, core]).astype(jnp.int32)

    grad_far = swap(gradients, "yh")
    grad_other = swap(gradients, "core")
    both = side_by_side(activations, basis_act)
    both_other = swap(both, "core")

    msg_near = near_messages(idx, gradients, gradients, grad_other)
    near_x = lax.all_to_all(msg_near, "x", 0, 0)
    proj = project(idx, (0, 0), after(gradients, both_other, msg_near), grad_other, basis_grad, None, f32)

    grad_far, proj = lax.optimization_barrier((grad_far, proj))
    grad_far_other = swap(grad_far, "core")
    both_far = swap(after(both, grad_far), "yh")
    msg_b = factor_messages(idx, gradients, grad_far, grad_far_other)
    got_b = along_x(msg_b)
    send_a, keep_a = near_sum_x(idx, after(near_x, *msg_b))
    proj, both_far = lax.optimization_barrier((proj, both_far, send_a))[:2]
    both_far_other = swap(both_far, "core")
    proj_grad = project(idx, (2, 0), grad_far, grad_far_other, basis_grad, proj, bf16)

    proj_act, act = act_parts(idx, (both, both_other, both_far, both_far_other))
    msg_e = scales_messages(idx, proj_grad, proj_act, act)
    got_e = along_x(msg_e)

    y_a = swap(send_a, "yl")
    send_b, keep_b = factor_sum_x(idx, [after(got_b[0], *msg_e)] + got_b[1:])
    y_b = swap(send_b, "yl")
    to_z = factor_sum_y(idx, keep_a, after(y_a, *got_e), keep_b, y_b)
    z_cov = lax.all_to_all(to_z, "z", 0, 0)
    grad_factor = factor_sum_z(z_cov)

    send_e, keep_e, keep_act = scales_sum_x(idx, [after(got_e[0], to_z)] + got_e[1:])
    y_e = swap(send_e, "yl")
    z_e = lax.all_to_all(after(scales_sum_y(idx, keep_e, keep_act, y_e), z_cov), "z", 0, 0)
    scales, act_factor = scales_sum_z(z_e)
    eigen_scales = lax.ppermute(scales, ("z", "yh", "core"), scales_places())
    return act_factor, grad_factor, eigen_scales


def solution(mesh):
    fine = Mesh(mesh.devices.reshape(SIZES), AXES)
    return jax.shard_map(
        on_device,
        mesh=fine,
        in_specs=(P(SAMP, CHAN), P(SAMP, CHAN), P(None, CHAN), P(None, CHAN)),
        out_specs=(P(SAMP, CHAN), P(SAMP, CHAN), P(SAMP, CHAN)),
        check_vma=False,
    )
```

```python
import functools

import jax
import jax.numpy as jnp
from jax import lax
from jax.experimental import pallas as pl
from jax.experimental.pallas import tpu as pltpu
from jax.sharding import Mesh, PartitionSpec as P

AXES = ("z", "yl", "x", "yh", "core")
SIZES = (8, 2, 4, 2, 2)
SAMP = ("z", "yl", "x")
CHAN = ("yh", "core")
HW = 784
ROWS = 50176
BLOCK = 768
TILE = 48
HALF = 24
PAD = 16
QUARTER = 192
f32, bf16 = jnp.float32, jnp.bfloat16
VMEM = pl.BlockSpec(memory_space=pltpu.VMEM)
SMEM = pl.BlockSpec(memory_space=pltpu.SMEM)
PARAMS = pltpu.CompilerParams(vmem_limit_bytes=24 << 20)


def crossed(left, right):
    return lax.dot_general(
        left, right, (((0,), (0,)), ((), ())), preferred_element_type=f32
    )


def exponent_of(peak):
    e = jnp.floor(jnp.log2(jnp.maximum(peak, 1e-30))) + 1.0
    return jnp.clip(e, -100.0, 100.0)


def coded(value):
    second = value * value
    fourth = second * second
    eighth = fourth * fourth
    return jnp.where(value < 0, -eighth, eighth)


def decoded(code):
    wide = code.astype(f32)
    root = jnp.exp(0.125 * jnp.log(jnp.maximum(jnp.abs(wide), 1e-37)))
    return jnp.where(wide < 0, -root, root)


def scale_of(e):
    return jnp.exp2(14.0 - e)


def unscale_of(rows):
    return jnp.exp2(rows[0:1, 0:1].astype(f32) - 14.0)


def peak_of(value, peak):
    return jnp.maximum(peak, jnp.max(jnp.abs(value), axis=(0, 1), keepdims=True))


def spread(e, rows, width):
    return jnp.broadcast_to(e, (rows, width))


def call(kernel, name, out_shape, in_specs, scratch=(), flops=0, size=0):
    return pl.pallas_call(
        kernel,
        out_shape=out_shape,
        in_specs=in_specs,
        out_specs=jax.tree.map(lambda _: VMEM, out_shape),
        scratch_shapes=list(scratch),
        compiler_params=PARAMS,
        cost_estimate=pl.CostEstimate(flops=1, bytes_accessed=1, transcendentals=0),
        name=name,
    )


def shape(rows, columns=BLOCK, dtype=bf16):
    return jax.ShapeDtypeStruct((rows, columns), dtype)


def factor_kernel(idx, own, same, other, o0, o1, o2, o3, p):
    x, core = idx[2], idx[4]
    peak = jnp.zeros((1, 1), f32)
    for b, rows in enumerate((same, other)):
        for c in range(3):
            cols = slice(c * 256, (c + 1) * 256)
            tile = crossed(rows[...], own[:, cols]) * (1.0 / ROWS)
            p[b, :, cols] = tile
            peak = peak_of(tile, peak)
    e = exponent_of(peak)
    scale = scale_of(e)
    for d, out in enumerate((o0, o1, o2, o3)):
        to = lax.rem(x + d, 4)
        for b, slot in enumerate((core, 1 - core)):
            for hy in range(4):
                src = pl.multiple_of((hy * 4 + to) * TILE, TILE)
                dst = pl.multiple_of((slot * 4 + hy) * TILE, TILE)
                out[pl.ds(dst, TILE), :] = coded(p[b, pl.ds(src, TILE), :] * scale).astype(bf16)
        out[8 * TILE :, :] = spread(e, PAD, BLOCK).astype(bf16)


def factor_messages(idx, own, same, other):
    return call(
        factor_kernel,
        "factor",
        [shape(8 * TILE + PAD)] * 4,
        [SMEM] + [VMEM] * 3,
        [pltpu.VMEM((2, BLOCK, BLOCK), f32)],
    )(idx, own, same, other)


def factor_sum_x_kernel(idx, m0, m1, m2, m3, send, keep, held):
    yl = idx[1]
    factors = [unscale_of(m[8 * TILE :, 0:128]) for m in (m0, m1, m2, m3)]

    def total(b, y):
        rows = pl.ds(pl.multiple_of((b * 2 + y) * TILE, TILE), TILE)
        parts = [decoded(m[rows, :]) * u for m, u in zip((m0, m1, m2, m3), factors)]
        return (parts[0] + parts[1]) + (parts[2] + parts[3])

    peak = jnp.zeros((1, 1), f32)
    for b in range(4):
        keep[b * TILE : (b + 1) * TILE, :] = total(b, yl)
        out = total(b, 1 - yl)
        held[b * TILE : (b + 1) * TILE, :] = out
        peak = peak_of(out, peak)
    e = exponent_of(peak)
    send[0 : 4 * TILE, :] = coded(held[...] * scale_of(e)).astype(bf16)
    send[4 * TILE :, :] = spread(e, PAD, BLOCK).astype(bf16)


def factor_sum_x(idx, messages):
    return call(
        factor_sum_x_kernel,
        "factor_sum_x",
        [shape(4 * TILE + PAD), shape(4 * TILE, dtype=f32)],
        [SMEM] + [VMEM] * 4,
        [pltpu.VMEM((4 * TILE, BLOCK), f32)],
    )(idx, *messages)


def factor_sum_y_kernel(idx, keep_a, got_a, keep_b, got_b, out, held):
    yh = idx[3]
    peak = jnp.zeros((1, 1), f32)
    for keep, got, half in ((keep_a, got_a, yh), (keep_b, got_b, 1 - yh)):
        unscale = unscale_of(got[4 * TILE :, 0:128])
        for b in range(4):
            rows = slice(b * TILE, (b + 1) * TILE)
            tile = keep[rows, :] + decoded(got[rows, :]) * unscale
            held[half * 4 + b] = tile
            peak = peak_of(tile, peak)
    e = exponent_of(peak)
    scale = scale_of(e)
    for z in range(8):
        out[z, 0:TILE, :] = coded(held[z] * scale).astype(bf16)
        out[z, TILE:, :] = spread(e, PAD, BLOCK).astype(bf16)


def factor_sum_y(idx, keep_a, got_a, keep_b, got_b):
    return call(
        factor_sum_y_kernel,
        "factor_sum_y",
        jax.ShapeDtypeStruct((8, TILE + PAD, BLOCK), bf16),
        [SMEM] + [VMEM] * 4,
        [pltpu.VMEM((8, TILE, BLOCK), f32)],
    )(idx, keep_a, got_a, keep_b, got_b)


def factor_sum_z_kernel(m, out):
    total = jnp.zeros(out.shape, f32)
    for z in range(8):
        total = total + decoded(m[z, 0:TILE, :]) * unscale_of(m[z, TILE:, 0:128])
    out[...] = total


def factor_sum_z(messages):
    return call(factor_sum_z_kernel, "factor_sum_z", shape(TILE, dtype=f32), [VMEM])(messages)


def factor_parts(own, same, other, p):
    peak = jnp.zeros((1, 1), f32)
    for b, rows in enumerate((same, other)):
        for c in range(3):
            cols = slice(c * 256, (c + 1) * 256)
            tile = crossed(rows[...], own[:, cols]) * (1.0 / ROWS)
            p[b, :, cols] = tile
            peak = peak_of(tile, peak)
    return exponent_of(peak)


def near_kernel(idx, own, same, other, out, p):
    core = idx[4]
    e = factor_parts(own, same, other, p)
    scale = scale_of(e)
    for b, slot in enumerate((core, 1 - core)):
        for hyx in range(16):
            dst = pl.multiple_of((slot * 4 + hyx // 4) * TILE, TILE)
            src = slice(hyx * TILE, (hyx + 1) * TILE)
            out[hyx % 4, pl.ds(dst, TILE), :] = coded(p[b, src, :] * scale).astype(bf16)
    for x in range(4):
        out[x, 8 * TILE :, :] = spread(e, PAD, BLOCK).astype(bf16)


def near_messages(idx, own, same, other):
    return call(
        near_kernel,
        "near",
        jax.ShapeDtypeStruct((4, 8 * TILE + PAD, BLOCK), bf16),
        [SMEM] + [VMEM] * 3,
        [pltpu.VMEM((2, BLOCK, BLOCK), f32)],
    )(idx, own, same, other)


def near_sum_x_kernel(idx, m, send, keep, held):
    yl = idx[1]
    factors = [unscale_of(m[d, 8 * TILE :, 0:128]) for d in range(4)]

    def total(b, y):
        rows = pl.ds(pl.multiple_of((b * 2 + y) * TILE, TILE), TILE)
        parts = [decoded(m[d, rows, :]) * factors[d] for d in range(4)]
        return (parts[0] + parts[1]) + (parts[2] + parts[3])

    peak = jnp.zeros((1, 1), f32)
    for b in range(4):
        keep[b * TILE : (b + 1) * TILE, :] = total(b, yl)
        out = total(b, 1 - yl)
        held[b * TILE : (b + 1) * TILE, :] = out
        peak = peak_of(out, peak)
    e = exponent_of(peak)
    send[0 : 4 * TILE, :] = coded(held[...] * scale_of(e)).astype(bf16)
    send[4 * TILE :, :] = spread(e, PAD, BLOCK).astype(bf16)


def near_sum_x(idx, messages):
    return call(
        near_sum_x_kernel,
        "near_sum_x",
        [shape(4 * TILE + PAD), shape(4 * TILE, dtype=f32)],
        [SMEM, VMEM],
        [pltpu.VMEM((4 * TILE, BLOCK), f32)],
    )(idx, messages)


def proj_kernel(first, idx, a, b, basis, *rest):
    before, out = (None, rest[0]) if len(rest) == 1 else rest
    chan = idx[3] * 2 + idx[4]
    width = a.shape[1]
    flip, offset = first
    for c in range(3):
        cols = slice(c * 256, (c + 1) * 256)
        total = None if before is None else before[:, cols]
        for n, part in enumerate((a, b)):
            start = pl.multiple_of((chan ^ (flip + n)) * BLOCK + offset, 128)
            term = jnp.dot(part[...], basis[pl.ds(start, width), cols], preferred_element_type=f32)
            total = term if total is None else total + term
        out[:, cols] = total.astype(out.dtype)


def project(idx, first, a, b, basis, before, dtype):
    operands = (idx, a, b, basis) + (() if before is None else (before,))
    return call(
        functools.partial(proj_kernel, first),
        "project",
        shape(HW, dtype=dtype),
        [SMEM] + [VMEM] * (len(operands) - 1),
        flops=4 * HW * a.shape[1] * BLOCK,
        size=8 << 20,
    )(*operands)


def beside_kernel(act, basis, out):
    out[:, 0:QUARTER] = act[...]
    out[0:BLOCK, QUARTER:] = basis[...]
    out[BLOCK:, QUARTER:] = jnp.zeros((HW - BLOCK, QUARTER), bf16)


def side_by_side(act, basis):
    return call(beside_kernel, "beside", shape(HW, 2 * QUARTER), [VMEM] * 2)(act, basis)


def act_kernel(idx, b0, b1, b2, b3, pa, act, basis, part):
    chan = idx[3] * 2 + idx[4]
    blocks = (b0, b1, b2, b3)
    for m, block in enumerate(blocks):
        cols = slice(m * QUARTER, (m + 1) * QUARTER)
        basis[:, cols] = block[0:BLOCK, QUARTER:]
        part[cols, :] = crossed(block[:, 0:QUARTER], b0[:, 0:QUARTER]) * (1.0 / ROWS)
    for c in range(3):
        cols = slice(c * 256, (c + 1) * 256)
        total = None
        for m, block in enumerate(blocks):
            start = pl.multiple_of((chan ^ m) * QUARTER, 64)
            term = jnp.dot(
                block[:, 0:QUARTER],
                basis[pl.ds(start, QUARTER), cols],
                preferred_element_type=f32,
            )
            total = term if total is None else total + term
        pa[:, cols] = total.astype(bf16)
    for to in range(4):
        for y in range(2):
            for m in range(4):
                for h in range(2):
                    src = m * QUARTER + (h * 8 + y * 4 + to) * 12
                    dst = y * HALF + h * 12
                    act[to, dst : dst + 12, m * QUARTER : (m + 1) * QUARTER] = part[src : src + 12, :]


def act_parts(idx, blocks):
    return call(
        act_kernel,
        "act",
        [shape(HW), jax.ShapeDtypeStruct((4, 2 * HALF, BLOCK), f32)],
        [SMEM] + [VMEM] * 4,
        [pltpu.VMEM((BLOCK, BLOCK), bf16), pltpu.VMEM((BLOCK, QUARTER), f32)],
        flops=2 * HW * BLOCK * 960,
        size=4 << 20,
    )(idx, *blocks)


def scales_kernel(idx, pg, pa, act, o0, o1, o2, o3, p):
    x = idx[2]
    peak = jnp.zeros((1, 1), f32)
    for c in range(3):
        cols = slice(c * 256, (c + 1) * 256)
        tile = crossed(pg[...], pa[:, cols])
        tile = tile * tile * (1.0 / ROWS)
        p[:, cols] = tile
        peak = peak_of(tile, peak)
    e = exponent_of(peak)
    scale = scale_of(e)
    act_peak = jnp.zeros((1, 1), f32)
    for to in range(4):
        act_peak = peak_of(act[to], act_peak)
    act_e = exponent_of(act_peak)
    act_scale = scale_of(act_e)
    for d, out in enumerate((o0, o1, o2, o3)):
        to = lax.rem(x + d, 4)
        for hy in range(4):
            src = pl.multiple_of((hy * 4 + to) * TILE, TILE)
            out[hy * TILE : (hy + 1) * TILE, :] = coded(p[pl.ds(src, TILE), :] * scale).astype(bf16)
        out[4 * TILE : 5 * TILE, :] = coded(act[to] * act_scale).astype(bf16)
        out[5 * TILE :, :] = jnp.concatenate(
            [spread(e, 8, BLOCK), spread(act_e, 8, BLOCK)], axis=0
        ).astype(bf16)


def scales_messages(idx, pg, pa, act):
    return call(
        scales_kernel,
        "scales",
        [shape(5 * TILE + PAD)] * 4,
        [SMEM] + [VMEM] * 3,
        [pltpu.VMEM((BLOCK, BLOCK), f32)],
        flops=2 * HW * BLOCK * BLOCK,
        size=4 << 20,
    )(idx, pg, pa, act)


def scales_sum_x_kernel(idx, m0, m1, m2, m3, send, keep, keep_act, held, held_act):
    yl = idx[1]
    messages = (m0, m1, m2, m3)
    ends = [m[5 * TILE :, 0:128].astype(f32) for m in messages]
    factors = [unscale_of(end) for end in ends]
    act_factors = [unscale_of(end[8:, :]) for end in ends]

    def total(h, y):
        rows = pl.ds(pl.multiple_of((h * 2 + y) * TILE, TILE), TILE)
        parts = [decoded(m[rows, :]) * u for m, u in zip(messages, factors)]
        return (parts[0] + parts[1]) + (parts[2] + parts[3])

    peak = jnp.zeros((1, 1), f32)
    for h in range(2):
        keep[h * TILE : (h + 1) * TILE, :] = total(h, yl)
        out = total(h, 1 - yl)
        held[h * TILE : (h + 1) * TILE, :] = out
        peak = peak_of(out, peak)
    parts = [decoded(m[4 * TILE : 5 * TILE, :]) * u for m, u in zip(messages, act_factors)]
    held_act[...] = (parts[0] + parts[1]) + (parts[2] + parts[3])
    keep_act[...] = held_act[pl.ds(pl.multiple_of(yl * HALF, 8), HALF), :]
    out = held_act[pl.ds(pl.multiple_of((1 - yl) * HALF, 8), HALF), :]
    e = exponent_of(peak)
    act_e = exponent_of(peak_of(out, jnp.zeros((1, 1), f32)))
    send[0 : 2 * TILE, :] = coded(held[...] * scale_of(e)).astype(bf16)
    send[2 * TILE : 2 * TILE + 32, :] = jnp.concatenate(
        [coded(out * scale_of(act_e)), spread(e, 8, BLOCK)], axis=0
    ).astype(bf16)
    send[2 * TILE + 32 :, :] = spread(act_e, PAD, BLOCK).astype(bf16)


def scales_sum_x(idx, messages):
    return call(
        scales_sum_x_kernel,
        "scales_sum_x",
        [shape(2 * TILE + 32 + PAD), shape(2 * TILE, dtype=f32), shape(HALF, dtype=f32)],
        [SMEM] + [VMEM] * 4,
        [pltpu.VMEM((2 * TILE, BLOCK), f32), pltpu.VMEM((2 * HALF, BLOCK), f32)],
        size=2 << 20,
    )(idx, *messages)


def scales_sum_y_kernel(idx, keep, keep_act, got, *refs):
    outs, held = refs[:8], refs[8]
    chan = idx[3] * 2 + idx[4]
    end = got[2 * TILE : 2 * TILE + 32, :].astype(f32)
    act_end = got[2 * TILE + 32 :, 0:128].astype(f32)
    tile = keep[...] + decoded(got[0 : 2 * TILE, :]) * unscale_of(end[HALF:, :])
    act = keep_act[...] + decoded(end[0:HALF, :]) * unscale_of(act_end)
    e = exponent_of(peak_of(tile, jnp.zeros((1, 1), f32)))
    act_e = exponent_of(peak_of(act, jnp.zeros((1, 1), f32)))
    tile = coded(tile * scale_of(e)).astype(bf16)
    act = coded(act * scale_of(act_e))
    for h in range(2):
        for m in range(4):
            cols = slice(m * QUARTER, (m + 1) * QUARTER)
            held[h * 4 + (chan ^ m), 0:TILE, :] = tile[h * TILE : (h + 1) * TILE, cols]
            held[(chan ^ m) * 2 + h, TILE:, :] = jnp.concatenate(
                [act[h * 12 : (h + 1) * 12, cols], spread(e, 2, QUARTER), spread(act_e, 2, QUARTER)],
                axis=0,
            ).astype(bf16)
    for d, out in enumerate(outs):
        out[...] = held[lax.rem(idx[0] + d, 8)]


def scales_sum_y(idx, keep, keep_act, got):
    return call(
        scales_sum_y_kernel,
        "scales_sum_y",
        [shape(TILE + 16, QUARTER)] * 8,
        [SMEM] + [VMEM] * 3,
        [pltpu.VMEM((8, TILE + 16, QUARTER), bf16)],
    )(idx, keep, keep_act, got)


def scales_sum_z_kernel(*refs):
    messages, (out, act) = refs[:8], refs[8:]
    total = jnp.zeros((TILE, QUARTER), f32)
    total_act = jnp.zeros((12, QUARTER), f32)
    for m in messages:
        end = m[TILE:, :].astype(f32)
        total = total + decoded(m[0:TILE, :]) * unscale_of(end[12:14, :])
        total_act = total_act + decoded(end[0:12, :]) * unscale_of(end[14:16, :])
    out[...] = total
    act[...] = total_act


def scales_sum_z(messages):
    return call(
        scales_sum_z_kernel,
        "scales_sum_z",
        [shape(TILE, QUARTER, f32), shape(12, QUARTER, f32)],
        [VMEM] * 8,
    )(*messages)


def after(value, *earlier):
    return lax.optimization_barrier((value,) + earlier)[0]


def swap(value, axis):
    return lax.ppermute(value, axis, [(0, 1), (1, 0)])


def along_x(messages):
    return [messages[0]] + [
        lax.ppermute(messages[d], "x", [(i, (i + d) % 4) for i in range(4)]) for d in (1, 3, 2)
    ]


def along_z(messages):
    return [messages[0]] + [
        lax.ppermute(messages[d], "z", [(i, (i + d) % 8) for i in range(8)])
        for d in (4, 3, 5, 2, 6, 1, 7)
    ]


def scales_places():
    return [
        (z * 4 + k, (2 * k + z // 4) * 4 + z % 4) for z in range(8) for k in range(4)
    ]


def on_device(activations, gradients, basis_act, basis_grad):
    z, yl, x, yh, core = [lax.axis_index(a) for a in AXES]
    idx = jnp.stack([z, yl, x, yh, core]).astype(jnp.int32)

    grad_far = swap(gradients, "yh")
    grad_other = swap(gradients, "core")
    both = side_by_side(activations, basis_act)
    both_other = swap(both, "core")

    msg_near = near_messages(idx, gradients, gradients, grad_other)
    near_x = lax.all_to_all(msg_near, "x", 0, 0)
    proj = project(idx, (0, 0), after(gradients, both_other, msg_near), grad_other, basis_grad, None, f32)

    grad_far, proj = lax.optimization_barrier((grad_far, proj))
    grad_far_other = swap(grad_far, "core")
    both_far = swap(after(both, grad_far), "yh")
    msg_b = factor_messages(idx, gradients, grad_far, grad_far_other)
    got_b = along_x(msg_b)
    send_a, keep_a = near_sum_x(idx, after(near_x, *msg_b))
    proj, both_far = lax.optimization_barrier((proj, both_far, send_a))[:2]
    both_far_other = swap(both_far, "core")
    proj_grad = project(idx, (2, 0), grad_far, grad_far_other, basis_grad, proj, bf16)

    proj_act, act = act_parts(idx, (both, both_other, both_far, both_far_other))
    msg_e = scales_messages(idx, proj_grad, proj_act, act)
    got_e = along_x(msg_e)

    y_a = swap(send_a, "yl")
    send_b, keep_b = factor_sum_x(idx, [after(got_b[0], *msg_e)] + got_b[1:])
    y_b = swap(send_b, "yl")
    to_z = factor_sum_y(idx, keep_a, after(y_a, *got_e), keep_b, y_b)
    z_cov = lax.all_to_all(to_z, "z", 0, 0)
    grad_factor = factor_sum_z(z_cov)

    send_e, keep_e, keep_act = scales_sum_x(idx, [after(got_e[0], to_z)] + got_e[1:])
    y_e = swap(send_e, "yl")
    scales, act_factor = scales_sum_z(along_z(scales_sum_y(idx, keep_e, keep_act, y_e)))
    eigen_scales = lax.ppermute(after(scales, z_cov), ("z", "yh", "core"), scales_places())
    return act_factor, grad_factor, eigen_scales


def solution(mesh):
    fine = Mesh(mesh.devices.reshape(SIZES), AXES)
    return jax.shard_map(
        on_device,
        mesh=fine,
        in_specs=(P(SAMP, CHAN), P(SAMP, CHAN), P(None, CHAN), P(None, CHAN)),
        out_specs=(P(SAMP, CHAN), P(SAMP, CHAN), P(SAMP, CHAN)),
        check_vma=False,
    )
```
